512 devices in a mesh: prompt: 8 (over y), resp: 64 (over z, x, core).
Axes of the slice: x: 4, y: 8, z: 8, core: 2. Of those that a mesh axis runs over, the one named last changes fastest.
Arguments:
- queries: bfloat16 [8, 64, 256, 2048], P('prompt', 'resp')
- resp_kv: bfloat16 [8, 64, 256, 1024], P('prompt', 'resp')
- out_grad: bfloat16 [8, 64, 256, 2048], P('prompt', 'resp'), may hold values from -6 to 6
- prompt_kv: bfloat16 [64, 128, 1024], P('resp', 'prompt'), may hold values from -6 to 6
- prompt_of: int32 [64], replicated, may hold values from 0 to 63, as said below
- lengths: int32 [8, 64], P('prompt', 'resp'), may hold values from 1 to 2
Outputs:
- query_grad: bfloat16 [8, 64, 256, 2048], P('prompt', 'resp')
- resp_kv_grad: bfloat16 [8, 64, 256, 1024], P('prompt', 'resp')
- prompt_kv_grad: float32 [64, 128, 1024], P('resp', 'prompt')
The draws below stay inside these ranges and needn't reach their ends.
Inputs may be any that keep to these rules, and one draw needn't show every extreme that they name: The cyclic distance between b and prompt_of[b] (mod 64) is at most 3; it is 3 on both sides for some b.
All inputs are finite; a program needn't handle non-finite values.
Results may differ from the reference program's by a relative error of at most 0.024.
Values may be sent and summed in bfloat16 or wider, within the bound.
A program may use at most 64 MiB of HBM per device.

```python
import jax
import jax.numpy as jnp
from jax import lax

QH = 16
KVH = 4
HD = 128
BLOCK = 128
RBLK = 2
REACH = 3
RLEN = 256
PLEN = 128
NPROMPTS = 64
KVW = 512
QW = 2048
N_PROMPT = 8
N_RESP = 64


def draw_resp_kv(key, part):
    key = jax.random.fold_in(key, 11)
    pieces = jnp.clip(jax.random.normal(key, (N_PROMPT, N_RESP, RLEN, 2, KVH, HD), jnp.float32), -5.0, 5.0)
    keys_part = pieces[:, :, :, 0]
    values_part = pieces[:, :, :, 1]
    whole = jnp.concatenate([keys_part.reshape(N_PROMPT, N_RESP, RLEN, KVH * HD), values_part.reshape(N_PROMPT, N_RESP, RLEN, KVH * HD)], axis=-1)
    return whole.astype(jnp.bfloat16)


def draw_queries(key, part):
    key = jax.random.fold_in(key, 12)
    query_part = jnp.clip(jax.random.normal(key, (N_PROMPT, N_RESP, RLEN, QH, HD), jnp.float32), -5.0, 5.0)
    return query_part.reshape(N_PROMPT, N_RESP, RLEN, QH * HD).astype(jnp.bfloat16)


def draw_prompt_of(key, part):
    key = jax.random.fold_in(key, 21)
    key_a, key_b = jax.random.split(key, 2)
    offsets = jax.random.randint(key_a, (N_RESP,), -REACH, REACH + 1)
    keeping = jax.random.randint(key_b, (N_RESP,), 0, 2)
    offsets = offsets * keeping
    half = N_RESP // 2
    offsets = offsets.at[(N_RESP - 1 + REACH) % N_RESP].set(REACH)
    offsets = offsets.at[half - 1 - REACH].set(-REACH)
    offsets = offsets.at[half + 1].set(1)
    columns = jnp.arange(N_RESP, dtype=jnp.int32)
    return ((columns - offsets) % N_RESP).astype(jnp.int32)


def draw_lengths(key, part):
    key = jax.random.fold_in(key, 31)
    key_a, key_b, key_c = jax.random.split(key, 3)
    count = N_PROMPT * N_RESP
    blocks = jax.random.randint(key_a, (count,), 1, RBLK + 1)
    first = jax.random.randint(key_b, (), 0, count)
    second = (first + 1 + jax.random.randint(key_c, (), 0, count - 1)) % count
    blocks = blocks.at[first].set(RBLK)
    blocks = blocks.at[second].set(1)
    return blocks.reshape(N_PROMPT, N_RESP).astype(jnp.int32)


def block_levels(stream_key, extent, cuts, low, top_value):
    loudness, own = 1.0, jax.random.fold_in(stream_key, 6)
    for axis_at, parts in cuts:
        steps = jnp.exp(jax.random.uniform(jax.random.fold_in(own, axis_at), (parts,), jnp.float32, low / len(cuts), top_value / len(cuts)))
        loudness = loudness * jnp.repeat(steps, extent[axis_at] // parts).reshape([-1 if axis == axis_at else 1 for axis in range(len(extent))])
    return loudness


def noise(rng, dims, spread, most, shards=(), kind=jnp.bfloat16):
    entries = spread * jax.random.normal(rng, dims, jnp.float32)
    if shards:
        entries = entries * block_levels(rng, dims, shards, -0.22, 0.18)
    return jnp.clip(entries, -most, most).astype(kind)


def setup_inputs(seed: int = 0) -> dict:
    splits = jax.random.split(jax.random.key(seed), 7)
    queries = draw_queries(jax.random.fold_in(splits[6], 71), 0)
    resp_kv = draw_resp_kv(jax.random.fold_in(splits[6], 71), 0)
    out_grad = noise(splits[2], (N_PROMPT, N_RESP, RLEN, QW), 1.0, 6.0, ((0, 8), (1, 64)))
    prompt_kv = noise(splits[3], (NPROMPTS, PLEN, 2 * KVW), 1.0, 6.0, ((0, 64), (1, 8)))
    prompt_of = draw_prompt_of(jax.random.fold_in(splits[6], 71), 0)
    lengths = draw_lengths(jax.random.fold_in(splits[6], 71), 0)
    return dict(queries=queries, resp_kv=resp_kv, out_grad=out_grad, prompt_kv=prompt_kv, prompt_of=prompt_of, lengths=lengths)


masked_value = -1.0e30


def slot_grads(query_rows, resp_rows, grad_rows, blocks, prompt_rows):
    groups = QH // KVH
    softmax_scale = HD ** -0.5
    row_index = jnp.arange(RLEN, dtype=jnp.int32)
    live_rows = row_index < blocks * BLOCK
    masked_grad = jnp.where(live_rows[:, None], grad_rows, jnp.zeros_like(grad_rows))
    keys_all = jnp.concatenate([prompt_rows[:, :KVW], resp_rows[:, :KVW]], axis=0)
    values_all = jnp.concatenate([prompt_rows[:, KVW:], resp_rows[:, KVW:]], axis=0)
    query_heads = query_rows.reshape(RLEN, KVH, groups, HD).astype(jnp.float32)
    grad_heads = masked_grad.reshape(RLEN, KVH, groups, HD).astype(jnp.float32)
    key_heads = keys_all.reshape(PLEN + RLEN, KVH, HD).astype(jnp.float32)
    value_heads = values_all.reshape(PLEN + RLEN, KVH, HD).astype(jnp.float32)
    score = jnp.einsum("rkgd,tkd->kgrt", query_heads, key_heads) * softmax_scale
    key_index = jnp.arange(PLEN + RLEN, dtype=jnp.int32)
    visible = (key_index[None, :] < PLEN) | (key_index[None, :] - PLEN <= row_index[:, None])
    score = jnp.where(visible[None, None], score, masked_value)
    top_score = jnp.max(score, axis=-1, keepdims=True)
    expd = jnp.exp(score - top_score)
    prob = expd / jnp.sum(expd, axis=-1, keepdims=True)
    prob_low = prob.astype(jnp.bfloat16).astype(jnp.float32)
    attn_out = jnp.einsum("kgrt,tkd->rkgd", prob_low, value_heads).astype(jnp.bfloat16)
    row_delta = jnp.sum(grad_heads * attn_out.astype(jnp.float32), axis=-1)
    prob_grad = jnp.einsum("rkgd,tkd->kgrt", grad_heads, value_heads)
    score_grad = (prob * (prob_grad - jnp.transpose(row_delta, (1, 2, 0))[..., None])).astype(jnp.bfloat16).astype(jnp.float32)
    query_grad = (jnp.einsum("kgrt,tkd->rkgd", score_grad, key_heads) * softmax_scale).astype(jnp.bfloat16)
    key_grad = jnp.einsum("kgrt,rkgd->tkd", score_grad, query_heads) * softmax_scale
    value_grad = jnp.einsum("kgrt,rkgd->tkd", prob_low, grad_heads)
    key_grad = key_grad.reshape(PLEN + RLEN, KVW)
    value_grad = value_grad.reshape(PLEN + RLEN, KVW)
    resp_grad = jnp.concatenate([key_grad[PLEN:], value_grad[PLEN:]], axis=1).astype(jnp.bfloat16)
    prompt_grad = jnp.concatenate([key_grad[:PLEN], value_grad[:PLEN]], axis=1)
    return query_grad.reshape(RLEN, QW), resp_grad, prompt_grad


def reference(queries, resp_kv, out_grad, prompt_kv, prompt_of, lengths):
    slots = N_PROMPT * N_RESP
    slot_prompt = jnp.tile(prompt_of, N_PROMPT).astype(jnp.int32)
    flat_query = queries.reshape(slots, RLEN, QW)
    flat_resp = resp_kv.reshape(slots, RLEN, 2 * KVW)
    flat_grad = out_grad.reshape(slots, RLEN, QW)
    flat_len = lengths.reshape(slots).astype(jnp.int32)

    def one_slot(carry, items):
        query_rows, resp_rows, grad_rows, blocks, which = items
        prompt_rows = lax.dynamic_index_in_dim(prompt_kv, which, 0, keepdims=False)
        query_grad, resp_grad, prompt_grad = slot_grads(query_rows, resp_rows, grad_rows, blocks, prompt_rows)
        carry = carry.at[which].add(prompt_grad)
        return carry, (query_grad, resp_grad)

    start = jnp.zeros((NPROMPTS, PLEN, 2 * KVW), jnp.float32)
    total, outputs = lax.scan(one_slot, start, (flat_query, flat_resp, flat_grad, flat_len, slot_prompt))
    query_grad = outputs[0].reshape(N_PROMPT, N_RESP, RLEN, QW)
    resp_grad = outputs[1].reshape(N_PROMPT, N_RESP, RLEN, 2 * KVW)
    return query_grad, resp_grad, total
```

```python
import functools
import math

import jax
import jax.numpy as jnp
from jax import lax
from jax.experimental import pallas as pl
from jax.experimental.pallas import tpu as pltpu
from jax.sharding import PartitionSpec as P

QH = 16
KVH = 4
GROUPS = QH // KVH
HD = 128
BLOCK = 128
REACH = 3
RLEN = 256
PLEN = 128
KVW = KVH * HD
QW = QH * HD
HALF = GROUPS * BLOCK
LANES = 2 * HALF
SCALE = HD**-0.5
LOG_SCALE = SCALE * math.log2(math.e)
STRIDES = (-3, 3, -2, 2, -1, 1)
MESH = pl.DeviceIdType.MESH
F32 = jnp.float32
BF16 = jnp.bfloat16
LOWEST = -3.0e38


def dot_t(a, b):
    return lax.dot_general(a, b, (((1,), (1,)), ((), ())), preferred_element_type=F32)


def dot_n(a, b):
    return lax.dot_general(a, b, (((1,), (0,)), ((), ())), preferred_element_type=F32)


def dot_l(a, b):
    return lax.dot_general(a, b, (((0,), (0,)), ((), ())), preferred_element_type=F32)


def head_rows(ref, head):
    parts = []
    for half in range(2):
        for group in range(GROUPS):
            columns = pl.ds(pl.multiple_of(head * HALF, HALF) + group * HD, HD)
            parts.append(ref[pl.ds(half * BLOCK, BLOCK), columns])
    return jnp.concatenate(parts, axis=0)


def columns_of(head, first):
    return pl.ds(pl.multiple_of(head * HD, HD) + first, HD)


def kernel(
    lengths_ref,
    owner_ref,
    q_hbm,
    kv_hbm,
    g_hbm,
    pkv_hbm,
    qg_hbm,
    rg_hbm,
    pg_hbm,
    q_ref,
    kv_ref,
    g_ref,
    land,
    gath,
    prob_resp,
    back_resp,
    stats,
    sg_prompt,
    grads,
    sums_in,
    sum_out,
    sum_land,
    qg_ref,
    rg_ref,
    pg_ref,
    in_sem,
    out_sem,
    own_sem,
    s1,
    r1,
    s2,
    r2,
    s3,
    r3,
    s4,
    r4,
):
    row = lax.axis_index("prompt")
    column = lax.axis_index("resp")
    n_row = lax.axis_size("prompt")
    n_col = lax.axis_size("resp")

    def beside(stride):
        return (row, lax.rem(column + stride + n_col, n_col))

    def above(step):
        return (lax.rem(row + step, n_row), column)

    loads = []
    for index, (source, target) in enumerate(((kv_hbm, kv_ref), (q_hbm, q_ref), (g_hbm, g_ref))):
        loads.append(pltpu.make_async_copy(source.at[0, 0], target, in_sem.at[index]))
    own = pltpu.make_async_copy(pkv_hbm.at[0], land.at[REACH], own_sem)

    barrier = pltpu.get_barrier_semaphore()
    for stride in STRIDES:
        pl.semaphore_signal(barrier, inc=1, device_id=beside(stride), device_id_type=MESH)
    for step in range(1, n_row):
        pl.semaphore_signal(barrier, inc=1, device_id=above(step), device_id_type=MESH)
    for load in loads:
        load.start()
    own.start()
    pl.semaphore_wait(barrier, len(STRIDES) + n_row - 1)

    to_readers = []
    for index, stride in enumerate(STRIDES):
        to_readers.append(
            pltpu.make_async_remote_copy(
                src_ref=pkv_hbm.at[0],
                dst_ref=land.at[REACH + stride],
                send_sem=s1.at[index],
                recv_sem=r1.at[index],
                device_id=beside(stride),
                device_id_type=MESH,
            )
        )
    for copy in to_readers:
        copy.start()

    blocks = lengths_ref[0, 0]
    key_at = lax.broadcasted_iota(jnp.int32, (BLOCK, HALF), 0)
    lane_at = lax.broadcasted_iota(jnp.int32, (BLOCK, HALF), 1)
    seen = key_at <= lax.rem(lane_at, BLOCK)

    def response(head, carry):
        span = pl.ds(pl.multiple_of(head * HALF, HALF), HALF)
        high = g_ref[pl.ds(BLOCK, BLOCK), span]
        g_ref[pl.ds(BLOCK, BLOCK), span] = jnp.where(blocks > 1, high, jnp.zeros_like(high))
        queries = head_rows(q_ref, head)
        out_grads = head_rows(g_ref, head)
        keys = kv_ref[:, columns_of(head, 0)]
        values = kv_ref[:, columns_of(head, KVW)]
        score0 = dot_t(keys[:BLOCK], queries)
        score1 = dot_t(keys[BLOCK:], queries[HALF:])
        low = jnp.where(seen, score0[:, :HALF], LOWEST)
        high0 = score0[:, HALF:]
        high1 = jnp.where(seen, score1, LOWEST)
        top_low = jnp.max(low, axis=0, keepdims=True) * LOG_SCALE
        top_high = (
            jnp.maximum(jnp.max(high0, axis=0, keepdims=True), jnp.max(high1, axis=0, keepdims=True))
            * LOG_SCALE
        )
        low = jnp.exp2(low * LOG_SCALE - top_low)
        high0 = jnp.exp2(high0 * LOG_SCALE - top_high)
        high1 = jnp.exp2(high1 * LOG_SCALE - top_high)
        mass_low = jnp.sum(low, axis=0, keepdims=True)
        mass_high = jnp.sum(high0, axis=0, keepdims=True) + jnp.sum(high1, axis=0, keepdims=True)
        low = low * (1.0 / mass_low)
        inverse = 1.0 / mass_high
        high0 = high0 * inverse
        high1 = high1 * inverse
        back0 = dot_t(values[:BLOCK], out_grads)
        back1 = dot_t(values[BLOCK:], out_grads[HALF:])
        delta_low = jnp.sum(low * back0[:, :HALF], axis=0, keepdims=True)
        delta_high = jnp.sum(high0 * back0[:, HALF:], axis=0, keepdims=True) + jnp.sum(
            high1 * back1, axis=0, keepdims=True
        )
        prob_resp[head, 0] = low
        prob_resp[head, 1] = high0
        prob_resp[head, 2] = high1
        back_resp[head, 0] = back0[:, :HALF]
        back_resp[head, 1] = back0[:, HALF:]
        back_resp[head, 2] = back1
        stats[head, 0:1] = jnp.concatenate([top_low, top_high], axis=1)
        stats[head, 1:2] = jnp.concatenate([mass_low, mass_high], axis=1)
        stats[head, 2:3] = jnp.concatenate([delta_low, delta_high], axis=1)
        return carry

    for load in loads:
        load.wait()
    lax.fori_loop(0, KVH // 2, response, 0)

    own.wait()
    for copy in to_readers:
        copy.wait()
    wanted = owner_ref[column]
    offset = lax.rem(column - wanted + n_col + REACH, n_col)
    mine = pl.ds(pl.multiple_of(row * 16, 16), 16)
    gath[mine] = land[jnp.minimum(offset, 2 * REACH)]
    spread = []
    for part in range(2):
        for step in (4, 3, 5, 2, 6, 1, 7):
            block = gath.at[mine, pl.ds(part * KVW, KVW)]
            spread.append(
                pltpu.make_async_remote_copy(
                    src_ref=block,
                    dst_ref=block,
                    send_sem=s2.at[part, step],
                    recv_sem=r2.at[part, step],
                    device_id=above(step),
                    device_id_type=MESH,
                )
            )
    for copy in spread:
        copy.start()
    lax.fori_loop(KVH // 2, KVH, response, 0)
    for copy in spread:
        copy.wait()

    def to_row(head, step):
        target = lax.rem(row + step, n_row)
        return pltpu.make_async_remote_copy(
            src_ref=grads.at[head, pl.ds(pl.multiple_of(target * 16, 16), 16)],
            dst_ref=sums_in.at[step, head],
            send_sem=s3.at[step],
            recv_sem=r3.at[step],
            device_id=above(step),
            device_id_type=MESH,
        )

    def prompt(head, carry):
        queries = head_rows(q_ref, head)
        out_grads = head_rows(g_ref, head)
        keys = gath[:, columns_of(head, 0)]
        values = gath[:, columns_of(head, KVW)]
        score = dot_t(keys, queries)
        top_resp = stats[head, 0:1]
        top = jnp.maximum(jnp.max(score, axis=0, keepdims=True) * LOG_SCALE, top_resp)
        prob = jnp.exp2(score * LOG_SCALE - top)
        mass_resp = jnp.exp2(top_resp - top) * stats[head, 1:2]
        inverse = 1.0 / (mass_resp + jnp.sum(prob, axis=0, keepdims=True))
        share = mass_resp * inverse
        prob = prob * inverse
        back = dot_t(values, out_grads)
        delta = share * stats[head, 2:3] + jnp.sum(prob * back, axis=0, keepdims=True)
        score_grad = (prob * (back - delta)).astype(BF16)
        grads[head, :, :HD] = (dot_n(score_grad, queries) * SCALE).astype(BF16)
        grads[head, :, HD:] = dot_n(prob.astype(BF16), out_grads).astype(BF16)
        sg_prompt[head] = score_grad
        stats[head, 3:4] = share
        stats[head, 4:5] = delta
        for step in (4, 3, 5, 2, 6, 1, 7):
            to_row(head, step).start()
        return carry

    lax.fori_loop(0, KVH, prompt, 0)

    def finish(head, carry):
        queries = head_rows(q_ref, head)
        out_grads = head_rows(g_ref, head)
        keys = kv_ref[:, columns_of(head, 0)]
        prompt_keys = gath[:, columns_of(head, 0)]
        share = stats[head, 3:4]
        delta = stats[head, 4:5]
        low = prob_resp[head, 0] * share[:, :HALF]
        high0 = prob_resp[head, 1] * share[:, HALF:]
        high1 = prob_resp[head, 2] * share[:, HALF:]
        sg_low = (low * (back_resp[head, 0] - delta[:, :HALF])).astype(BF16)
        sg_high0 = (high0 * (back_resp[head, 1] - delta[:, HALF:])).astype(BF16)
        sg_high1 = (high1 * (back_resp[head, 2] - delta[:, HALF:])).astype(BF16)
        sg0 = jnp.concatenate([sg_low, sg_high0], axis=1)
        pr0 = jnp.concatenate([low.astype(BF16), high0.astype(BF16)], axis=1)
        key_at = columns_of(head, 0)
        value_at = columns_of(head, KVW)
        rg_ref[pl.ds(0, BLOCK), key_at] = (dot_n(sg0, queries) * SCALE).astype(BF16)
        rg_ref[pl.ds(BLOCK, BLOCK), key_at] = (dot_n(sg_high1, queries[HALF:]) * SCALE).astype(BF16)
        rg_ref[pl.ds(0, BLOCK), value_at] = dot_n(pr0, out_grads).astype(BF16)
        rg_ref[pl.ds(BLOCK, BLOCK), value_at] = dot_n(high1.astype(BF16), out_grads[HALF:]).astype(BF16)
        sgp = sg_prompt[head]
        grad_low = dot_l(
            jnp.concatenate([sgp[:, :HALF], sg_low], axis=0),
            jnp.concatenate([prompt_keys, keys[:BLOCK]], axis=0),
        )
        grad_high = dot_l(
            jnp.concatenate([sgp[:, HALF:], sg_high0, sg_high1], axis=0),
            jnp.concatenate([prompt_keys, keys], axis=0),
        )
        for half, grad in enumerate((grad_low, grad_high)):
            grad = (grad * SCALE).astype(BF16)
            for group in range(GROUPS):
                at = pl.ds(pl.multiple_of(head * HALF, HALF) + group * HD, HD)
                qg_ref[pl.ds(half * BLOCK, BLOCK), at] = grad[group * BLOCK : (group + 1) * BLOCK]
        return carry

    lax.fori_loop(0, KVH, finish, 0)
    stores = [
        pltpu.make_async_copy(qg_ref, qg_hbm.at[0, 0], out_sem.at[0]),
        pltpu.make_async_copy(rg_ref, rg_hbm.at[0, 0], out_sem.at[1]),
    ]
    for store in stores:
        store.start()

    total = grads[:, mine].astype(F32)
    for step in range(1, n_row):
        pltpu.make_async_remote_copy(
            src_ref=sums_in.at[step],
            dst_ref=sums_in.at[step],
            send_sem=s3.at[step],
            recv_sem=r3.at[step],
            device_id=above(step),
            device_id_type=MESH,
        ).wait()
        total = total + sums_in[step].astype(F32)
    sum_out[...] = total.astype(BF16)
    to_owners = []
    for index, stride in enumerate(STRIDES):
        to_owners.append(
            pltpu.make_async_remote_copy(
                src_ref=sum_out,
                dst_ref=sum_land.at[index],
                send_sem=s4.at[index],
                recv_sem=r4.at[index],
                device_id=beside(stride),
                device_id_type=MESH,
            )
        )
    for copy in to_owners:
        copy.start()
    total = jnp.where(wanted == column, total, 0.0)
    for index, stride in enumerate(STRIDES):
        to_owners[index].wait()
        reads = owner_ref[lax.rem(column - stride + n_col, n_col)] == column
        total = total + jnp.where(reads, sum_land[index].astype(F32), 0.0)
    for head in range(KVH):
        pg_ref[:, head * HD : (head + 1) * HD] = total[head, :, :HD]
        pg_ref[:, KVW + head * HD : KVW + (head + 1) * HD] = total[head, :, HD:]
    store = pltpu.make_async_copy(pg_ref, pg_hbm.at[0], out_sem.at[2])
    store.start()
    stores.append(store)
    for store in stores:
        store.wait()


def shards(queries, resp_kv, out_grad, prompt_kv, prompt_of, lengths):
    any_spec = pl.BlockSpec(memory_space=pl.ANY)
    smem_spec = pl.BlockSpec(memory_space=pltpu.SMEM)
    return pl.pallas_call(
        kernel,
        out_shape=(
            jax.ShapeDtypeStruct(queries.shape, BF16),
            jax.ShapeDtypeStruct(resp_kv.shape, BF16),
            jax.ShapeDtypeStruct(prompt_kv.shape, F32),
        ),
        in_specs=[smem_spec, smem_spec] + [any_spec] * 4,
        out_specs=(any_spec,) * 3,
        scratch_shapes=[
            pltpu.VMEM((RLEN, QW), BF16),
            pltpu.VMEM((RLEN, 2 * KVW), BF16),
            pltpu.VMEM((RLEN, QW), BF16),
            pltpu.VMEM((2 * REACH + 1, 16, 2 * KVW), BF16),
            pltpu.VMEM((PLEN, 2 * KVW), BF16),
            pltpu.VMEM((KVH, 3, BLOCK, HALF), F32),
            pltpu.VMEM((KVH, 3, BLOCK, HALF), F32),
            pltpu.VMEM((KVH, 8, LANES), F32),
            pltpu.VMEM((KVH, PLEN, LANES), BF16),
            pltpu.VMEM((KVH, PLEN, 2 * HD), BF16),
            pltpu.VMEM((8, KVH, 16, 2 * HD), BF16),
            pltpu.VMEM((KVH, 16, 2 * HD), BF16),
            pltpu.VMEM((2 * REACH, KVH, 16, 2 * HD), BF16),
            pltpu.VMEM((RLEN, QW), BF16),
            pltpu.VMEM((RLEN, 2 * KVW), BF16),
            pltpu.VMEM((16, 2 * KVW), F32),
            pltpu.SemaphoreType.DMA((3,)),
            pltpu.SemaphoreType.DMA((3,)),
            pltpu.SemaphoreType.DMA,
            pltpu.SemaphoreType.DMA((6,)),
            pltpu.SemaphoreType.DMA((6,)),
            pltpu.SemaphoreType.DMA((2, 8)),
            pltpu.SemaphoreType.DMA((2, 8)),
            pltpu.SemaphoreType.DMA((8,)),
            pltpu.SemaphoreType.DMA((8,)),
            pltpu.SemaphoreType.DMA((6,)),
            pltpu.SemaphoreType.DMA((6,)),
        ],
        compiler_params=pltpu.CompilerParams(
            collective_id=0, has_side_effects=True, vmem_limit_bytes=56 << 20
        ),
        name="slot_grads",
    )(lengths, prompt_of, queries, resp_kv, out_grad, prompt_kv)


def solution(mesh):
    return jax.shard_map(
        shards,
        mesh=mesh,
        in_specs=(
            P("prompt", "resp", None, None),
            P("prompt", "resp", None, None),
            P("prompt", "resp", None, None),
            P("resp", "prompt", None),
            P(),
            P("prompt", "resp"),
        ),
        out_specs=(
            P("prompt", "resp", None, None),
            P("prompt", "resp", None, None),
            P("resp", "prompt", None),
        ),
        check_vma=False,
    )
```

```python
import functools
import math

import jax
import jax.numpy as jnp
from jax import lax
from jax.experimental import pallas as pl
from jax.experimental.pallas import tpu as pltpu
from jax.sharding import PartitionSpec as P

QH = 16
KVH = 4
GROUPS = QH // KVH
HD = 128
BLOCK = 128
REACH = 3
RLEN = 256
PLEN = 128
KVW = KVH * HD
QW = QH * HD
HALF = GROUPS * BLOCK
LANES = 2 * HALF
SCALE = HD**-0.5
LOG_SCALE = SCALE * math.log2(math.e)
CHUNKS = 2
PER = KVH // CHUNKS
STRIDES = (-3, 3, -2, 2, -1, 1)
STEPS = (4, 3, 5, 2, 6, 1, 7)
MESH = pl.DeviceIdType.MESH
F32 = jnp.float32
BF16 = jnp.bfloat16
LOWEST = -3.0e38


def dot_t(a, b):
    return lax.dot_general(a, b, (((1,), (1,)), ((), ())), preferred_element_type=F32)


def dot_n(a, b):
    return lax.dot_general(a, b, (((1,), (0,)), ((), ())), preferred_element_type=F32)


def dot_l(a, b):
    return lax.dot_general(a, b, (((0,), (0,)), ((), ())), preferred_element_type=F32)


def head_rows(ref, head):
    parts = []
    for half in range(2):
        for group in range(GROUPS):
            columns = pl.ds(pl.multiple_of(head * HALF, HALF) + group * HD, HD)
            parts.append(ref[pl.ds(half * BLOCK, BLOCK), columns])
    return jnp.concatenate(parts, axis=0)


def columns_of(head, first):
    return pl.ds(pl.multiple_of(head * HD, HD) + first, HD)


def kernel(
    lengths_ref,
    owner_hbm,
    q_hbm,
    kv_hbm,
    g_hbm,
    pkv_hbm,
    qg_ref,
    rg_ref,
    pg_ref,
    owner_ref,
    q_ref,
    kv_ref,
    g_ref,
    own_ref,
    land0,
    land1,
    gath,
    prob_resp,
    back_resp,
    stats,
    sg_prompt,
    grads,
    sums_in,
    sum_out,
    sum_land,
    in_sem,
    s1,
    r1,
    s2,
    r2,
    s3,
    r3,
    s4,
    r4,
):
    land = (land0, land1)
    row = lax.axis_index("prompt")
    column = lax.axis_index("resp")
    n_row = lax.axis_size("prompt")
    n_col = lax.axis_size("resp")

    def beside(stride):
        return (row, lax.rem(column + stride + n_col, n_col))

    def above(step):
        return (lax.rem(row + step, n_row), column)

    def heads_of(chunk):
        return pl.ds(chunk * PER, PER)

    own = pltpu.make_async_copy(pkv_hbm.at[0], own_ref, in_sem.at[0])
    own.start()
    barrier = pltpu.get_barrier_semaphore()
    for stride in STRIDES:
        pl.semaphore_signal(barrier, inc=1, device_id=beside(stride), device_id_type=MESH)
    for step in STEPS:
        pl.semaphore_signal(barrier, inc=1, device_id=above(step), device_id_type=MESH)
    loads = []
    for source, target in (
        (owner_hbm, owner_ref),
        (kv_hbm.at[0, 0], kv_ref),
        (q_hbm.at[0, 0], q_ref),
        (g_hbm.at[0, 0], g_ref),
    ):
        loads.append(pltpu.make_async_copy(source, target, in_sem.at[len(loads) + 1]))
        loads[-1].start()
    own.wait()
    for head in range(KVH):
        part = land[head // PER].at[REACH, head % PER]
        part[:, :HD] = own_ref[:, head * HD : (head + 1) * HD]
        part[:, HD:] = own_ref[:, KVW + head * HD : KVW + (head + 1) * HD]
    pl.semaphore_wait(barrier, len(STRIDES) + n_row - 1)

    def to_reader(chunk, index):
        return pltpu.make_async_remote_copy(
            src_ref=land[chunk].at[REACH],
            dst_ref=land[chunk].at[REACH + STRIDES[index]],
            send_sem=s1.at[chunk, index],
            recv_sem=r1.at[chunk, index],
            device_id=beside(STRIDES[index]),
            device_id_type=MESH,
        )

    for chunk in range(CHUNKS):
        for index in range(len(STRIDES)):
            to_reader(chunk, index).start()
    for load in loads:
        load.wait()

    blocks = lengths_ref[0, 0]
    key_at = lax.broadcasted_iota(jnp.int32, (BLOCK, HALF), 0)
    lane_at = lax.broadcasted_iota(jnp.int32, (BLOCK, HALF), 1)
    seen = key_at <= lax.rem(lane_at, BLOCK)

    def response(head, carry):
        span = pl.ds(pl.multiple_of(head * HALF, HALF), HALF)
        high = g_ref[pl.ds(BLOCK, BLOCK), span]
        g_ref[pl.ds(BLOCK, BLOCK), span] = jnp.where(blocks > 1, high, jnp.zeros_like(high))
        queries = head_rows(q_ref, head)
        out_grads = head_rows(g_ref, head)
        keys = kv_ref[:, columns_of(head, 0)]
        values = kv_ref[:, columns_of(head, KVW)]
        score0 = dot_t(keys[:BLOCK], queries)
        score1 = dot_t(keys[BLOCK:], queries[HALF:])
        low = jnp.where(seen, score0[:, :HALF], LOWEST)
        high0 = score0[:, HALF:]
        high1 = jnp.where(seen, score1, LOWEST)
        top_low = jnp.max(low, axis=0, keepdims=True) * LOG_SCALE
        top_high = (
            jnp.maximum(jnp.max(high0, axis=0, keepdims=True), jnp.max(high1, axis=0, keepdims=True))
            * LOG_SCALE
        )
        low = jnp.exp2(low * LOG_SCALE - top_low)
        high0 = jnp.exp2(high0 * LOG_SCALE - top_high)
        high1 = jnp.exp2(high1 * LOG_SCALE - top_high)
        mass_low = jnp.sum(low, axis=0, keepdims=True)
        mass_high = jnp.sum(high0, axis=0, keepdims=True) + jnp.sum(high1, axis=0, keepdims=True)
        low = low * (1.0 / mass_low)
        inverse = 1.0 / mass_high
        high0 = high0 * inverse
        high1 = high1 * inverse
        back0 = dot_t(values[:BLOCK], out_grads)
        back1 = dot_t(values[BLOCK:], out_grads[HALF:])
        delta_low = jnp.sum(low * back0[:, :HALF], axis=0, keepdims=True)
        delta_high = jnp.sum(high0 * back0[:, HALF:], axis=0, keepdims=True) + jnp.sum(
            high1 * back1, axis=0, keepdims=True
        )
        prob_resp[head, 0] = low
        prob_resp[head, 1] = high0
        prob_resp[head, 2] = high1
        back_resp[head, 0] = back0[:, :HALF]
        back_resp[head, 1] = back0[:, HALF:]
        back_resp[head, 2] = back1
        stats[head, 0:1] = jnp.concatenate([top_low, top_high], axis=1)
        stats[head, 1:2] = jnp.concatenate([mass_low, mass_high], axis=1)
        stats[head, 2:3] = jnp.concatenate([delta_low, delta_high], axis=1)
        return carry

    lax.fori_loop(0, KVH, response, 0)

    wanted = owner_ref[column]
    offset = jnp.minimum(lax.rem(column - wanted + n_col + REACH, n_col), 2 * REACH)
    mine = pl.ds(pl.multiple_of(row * 16, 16), 16)

    def along(chunk, step):
        block = gath.at[heads_of(chunk), mine]
        return pltpu.make_async_remote_copy(
            src_ref=block,
            dst_ref=block,
            send_sem=s2.at[chunk, step],
            recv_sem=r2.at[chunk, step],
            device_id=above(step),
            device_id_type=MESH,
        )

    for chunk in range(CHUNKS):
        for index in range(len(STRIDES)):
            to_reader(chunk, index).wait_recv()
        gath[heads_of(chunk), mine] = land[chunk][offset]
        for step in STEPS:
            along(chunk, step).start()

    def to_row(chunk, step):
        target = lax.rem(row + step, n_row)
        return pltpu.make_async_remote_copy(
            src_ref=grads.at[heads_of(chunk), pl.ds(pl.multiple_of(target * 16, 16), 16)],
            dst_ref=sums_in.at[step, heads_of(chunk)],
            send_sem=s3.at[chunk, step],
            recv_sem=r3.at[chunk, step],
            device_id=above(step),
            device_id_type=MESH,
        )

    def prompt(head, carry):
        queries = head_rows(q_ref, head)
        out_grads = head_rows(g_ref, head)
        keys = gath[head, :, :HD]
        values = gath[head, :, HD:]
        score = dot_t(keys, queries)
        top_resp = stats[head, 0:1]
        top = jnp.maximum(jnp.max(score, axis=0, keepdims=True) * LOG_SCALE, top_resp)
        prob = jnp.exp2(score * LOG_SCALE - top)
        mass_resp = jnp.exp2(top_resp - top) * stats[head, 1:2]
        inverse = 1.0 / (mass_resp + jnp.sum(prob, axis=0, keepdims=True))
        share = mass_resp * inverse
        prob = prob * inverse
        back = dot_t(values, out_grads)
        delta = share * stats[head, 2:3] + jnp.sum(prob * back, axis=0, keepdims=True)
        score_grad = (prob * (back - delta)).astype(BF16)
        grads[head, :, :HD] = (dot_n(score_grad, queries) * SCALE).astype(BF16)
        grads[head, :, HD:] = dot_n(prob.astype(BF16), out_grads).astype(BF16)
        sg_prompt[head] = score_grad
        stats[head, 3:4] = share
        stats[head, 4:5] = delta
        return carry

    for chunk in range(CHUNKS):
        for step in STEPS:
            along(chunk, step).wait_recv()
        lax.fori_loop(chunk * PER, (chunk + 1) * PER, prompt, 0)
        for step in STEPS:
            to_row(chunk, step).start()

    def finish(head, carry):
        queries = head_rows(q_ref, head)
        out_grads = head_rows(g_ref, head)
        keys = kv_ref[:, columns_of(head, 0)]
        prompt_keys = gath[head, :, :HD]
        share = stats[head, 3:4]
        delta = stats[head, 4:5]
        low = prob_resp[head, 0] * share[:, :HALF]
        high0 = prob_resp[head, 1] * share[:, HALF:]
        high1 = prob_resp[head, 2] * share[:, HALF:]
        sg_low = (low * (back_resp[head, 0] - delta[:, :HALF])).astype(BF16)
        sg_high0 = (high0 * (back_resp[head, 1] - delta[:, HALF:])).astype(BF16)
        sg_high1 = (high1 * (back_resp[head, 2] - delta[:, HALF:])).astype(BF16)
        sg0 = jnp.concatenate([sg_low, sg_high0], axis=1)
        pr0 = jnp.concatenate([low.astype(BF16), high0.astype(BF16)], axis=1)
        key_at = columns_of(head, 0)
        value_at = columns_of(head, KVW)
        rg_ref[pl.ds(0, BLOCK), key_at] = (dot_n(sg0, queries) * SCALE).astype(BF16)
        rg_ref[pl.ds(BLOCK, BLOCK), key_at] = (dot_n(sg_high1, queries[HALF:]) * SCALE).astype(BF16)
        rg_ref[pl.ds(0, BLOCK), value_at] = dot_n(pr0, out_grads).astype(BF16)
        rg_ref[pl.ds(BLOCK, BLOCK), value_at] = dot_n(high1.astype(BF16), out_grads[HALF:]).astype(BF16)
        sgp = sg_prompt[head]
        grad_low = dot_l(
            jnp.concatenate([sgp[:, :HALF], sg_low], axis=0),
            jnp.concatenate([prompt_keys, keys[:BLOCK]], axis=0),
        )
        grad_high = dot_l(
            jnp.concatenate([sgp[:, HALF:], sg_high0, sg_high1], axis=0),
            jnp.concatenate([prompt_keys, keys], axis=0),
        )
        for half, grad in enumerate((grad_low, grad_high)):
            grad = (grad * SCALE).astype(BF16)
            for group in range(GROUPS):
                at = pl.ds(pl.multiple_of(head * HALF, HALF) + group * HD, HD)
                qg_ref[pl.ds(half * BLOCK, BLOCK), at] = grad[group * BLOCK : (group + 1) * BLOCK]
        return carry

    lax.fori_loop(0, KVH, finish, 0)

    def to_owner(chunk, index):
        return pltpu.make_async_remote_copy(
            src_ref=sum_out.at[heads_of(chunk)],
            dst_ref=sum_land.at[index, heads_of(chunk)],
            send_sem=s4.at[chunk, index],
            recv_sem=r4.at[chunk, index],
            device_id=beside(STRIDES[index]),
            device_id_type=MESH,
        )

    totals = []
    for chunk in range(CHUNKS):
        total = grads[heads_of(chunk), mine].astype(F32)
        for step in STEPS:
            to_row(chunk, step).wait_recv()
        for step in STEPS:
            total = total + sums_in[step, heads_of(chunk)].astype(F32)
        sum_out[heads_of(chunk)] = total.astype(BF16)
        for index in range(len(STRIDES)):
            to_owner(chunk, index).start()
        totals.append(jnp.where(wanted == column, total, 0.0))
    for chunk in range(CHUNKS):
        for index in range(len(STRIDES)):
            to_reader(chunk, index).wait_send()
        for step in STEPS:
            along(chunk, step).wait_send()
            to_row(chunk, step).wait_send()
    for chunk in range(CHUNKS):
        total = totals[chunk]
        for index in range(len(STRIDES)):
            to_owner(chunk, index).wait()
        for index, stride in enumerate(STRIDES):
            reads = owner_ref[lax.rem(column - stride + n_col, n_col)] == column
            total = total + jnp.where(reads, sum_land[index, heads_of(chunk)].astype(F32), 0.0)
        for at in range(PER):
            head = chunk * PER + at
            pg_ref[:, head * HD : (head + 1) * HD] = total[at, :, :HD]
            pg_ref[:, KVW + head * HD : KVW + (head + 1) * HD] = total[at, :, HD:]


def store_kernel(qg_ref, rg_ref, pg_ref, qg_hbm, rg_hbm, pg_hbm, sem):
    stores = [
        pltpu.make_async_copy(qg_ref, qg_hbm.at[0, 0], sem.at[0]),
        pltpu.make_async_copy(rg_ref, rg_hbm.at[0, 0], sem.at[1]),
        pltpu.make_async_copy(pg_ref, pg_hbm.at[0], sem.at[2]),
    ]
    for store in stores:
        store.start()
    for store in stores:
        store.wait()


def shards(queries, resp_kv, out_grad, prompt_kv, prompt_of, lengths):
    in_hbm = pl.BlockSpec(memory_space=pltpu.HBM)
    in_vmem = pl.BlockSpec(memory_space=pltpu.VMEM)
    operands = (lengths, prompt_of, queries, resp_kv, out_grad, prompt_kv)
    operands = (pltpu.with_memory_space_constraint(lengths, pltpu.SMEM),) + tuple(pltpu.with_memory_space_constraint(operand, pltpu.HBM) for operand in operands[1:])
    results = pl.pallas_call(
        kernel,
        out_shape=(
            pltpu.VMEM((RLEN, QW), BF16),
            pltpu.VMEM((RLEN, 2 * KVW), BF16),
            pltpu.VMEM((16, 2 * KVW), F32),
        ),
        in_specs=[pl.BlockSpec(memory_space=pltpu.SMEM)] + [in_hbm] * 5,
        out_specs=(in_vmem,) * 3,
        scratch_shapes=[
            pltpu.SMEM((64,), jnp.int32),
            pltpu.VMEM((RLEN, QW), BF16),
            pltpu.VMEM((RLEN, 2 * KVW), BF16),
            pltpu.VMEM((RLEN, QW), BF16),
            pltpu.VMEM((16, 2 * KVW), BF16),
            pltpu.VMEM((2 * REACH + 1, PER, 16, 2 * HD), BF16),
            pltpu.VMEM((2 * REACH + 1, PER, 16, 2 * HD), BF16),
            pltpu.VMEM((KVH, PLEN, 2 * HD), BF16),
            pltpu.VMEM((KVH, 3, BLOCK, HALF), F32),
            pltpu.VMEM((KVH, 3, BLOCK, HALF), F32),
            pltpu.VMEM((KVH, 8, LANES), F32),
            pltpu.VMEM((KVH, PLEN, LANES), BF16),
            pltpu.VMEM((KVH, PLEN, 2 * HD), BF16),
            pltpu.VMEM((8, KVH, 16, 2 * HD), BF16),
            pltpu.VMEM((KVH, 16, 2 * HD), BF16),
            pltpu.VMEM((2 * REACH, KVH, 16, 2 * HD), BF16),
            pltpu.SemaphoreType.DMA((6,)),
            pltpu.SemaphoreType.DMA((CHUNKS, 6)),
            pltpu.SemaphoreType.DMA((CHUNKS, 6)),
            pltpu.SemaphoreType.DMA((CHUNKS, 8)),
            pltpu.SemaphoreType.DMA((CHUNKS, 8)),
            pltpu.SemaphoreType.DMA((CHUNKS, 8)),
            pltpu.SemaphoreType.DMA((CHUNKS, 8)),
            pltpu.SemaphoreType.DMA((CHUNKS, 6)),
            pltpu.SemaphoreType.DMA((CHUNKS, 6)),
        ],
        compiler_params=pltpu.CompilerParams(
            collective_id=0, has_side_effects=True, vmem_limit_bytes=40 << 20
        ),
        name="slot_grads",
    )(*operands)
    results = [pltpu.with_memory_space_constraint(result, pltpu.VMEM) for result in results]
    return pl.pallas_call(
        store_kernel,
        out_shape=(
            jax.ShapeDtypeStruct(queries.shape, BF16),
            jax.ShapeDtypeStruct(resp_kv.shape, BF16),
            jax.ShapeDtypeStruct(prompt_kv.shape, F32),
        ),
        in_specs=[in_vmem] * 3,
        out_specs=(in_hbm,) * 3,
        scratch_shapes=[pltpu.SemaphoreType.DMA((3,))],
        name="store",
    )(*results)


def solution(mesh):
    return jax.shard_map(
        shards,
        mesh=mesh,
        in_specs=(
            P("prompt", "resp", None, None),
            P("prompt", "resp", None, None),
            P("prompt", "resp", None, None),
            P("resp", "prompt", None),
            P(),
            P("prompt", "resp"),
        ),
        out_specs=(
            P("prompt", "resp", None, None),
            P("prompt", "resp", None, None),
            P("resp", "prompt", None),
        ),
        check_vma=False,
    )
```

```python
import functools
import math

import jax
import jax.numpy as jnp
from jax import lax
from jax.experimental import pallas as pl
from jax.experimental.pallas import tpu as pltpu
from jax.sharding import PartitionSpec as P

QH = 16
KVH = 4
GROUPS = QH // KVH
HD = 128
BLOCK = 128
REACH = 3
RLEN = 256
PLEN = 128
KVW = KVH * HD
QW = QH * HD
HALF = GROUPS * BLOCK
LANES = 2 * HALF
SCALE = HD**-0.5
LOG_SCALE = SCALE * math.log2(math.e)
PROMPT_PARTS = ((0, 2), (2, 1), (3, 1))
GRAD_PARTS = ((0, 1), (1, 1), (2, 1), (3, 1))
SUM_PARTS = ((0, 2), (2, 2))
STRIDES = (-3, 3, -2, 2, -1, 1)
STEPS = (4, 3, 5, 2, 6, 1, 7)
NEAR = (1, 7, 2, 6)
MESH = pl.DeviceIdType.MESH
F32 = jnp.float32
BF16 = jnp.bfloat16
LOWEST = -3.0e38


def dot_t(a, b):
    return lax.dot_general(a, b, (((1,), (1,)), ((), ())), preferred_element_type=F32)


def dot_n(a, b):
    return lax.dot_general(a, b, (((1,), (0,)), ((), ())), preferred_element_type=F32)


def dot_l(a, b):
    return lax.dot_general(a, b, (((0,), (0,)), ((), ())), preferred_element_type=F32)


def head_rows(ref, head):
    parts = []
    for half in range(2):
        for group in range(GROUPS):
            first = head * HALF if isinstance(head, int) else pl.multiple_of(head * HALF, HALF)
            columns = pl.ds(first + group * HD, HD)
            parts.append(ref[pl.ds(half * BLOCK, BLOCK), columns])
    return jnp.concatenate(parts, axis=0)


def columns_of(head, first):
    return pl.ds(head * HD + first, HD) if isinstance(head, int) else pl.ds(pl.multiple_of(head * HD, HD) + first, HD)


def kernel(
    lengths_ref,
    owner_hbm,
    q_hbm,
    kv_hbm,
    g_hbm,
    pkv_hbm,
    qg_ref,
    rg_ref,
    pg_ref,
    owner_ref,
    q_ref,
    kv_ref,
    g_ref,
    own_ref,
    land,
    gath,
    prob_resp,
    back_resp,
    stats,
    sg_prompt,
    grads,
    sums_in,
    sum_out,
    sum_land,
    in_sem,
    near_sem,
    s1,
    r1,
    s2,
    r2,
    s3,
    r3,
    s4,
    r4,
):
    row = lax.axis_index("prompt")
    column = lax.axis_index("resp")
    n_row = lax.axis_size("prompt")
    n_col = lax.axis_size("resp")

    def beside(stride):
        return (row, lax.rem(column + stride + n_col, n_col))

    def above(step):
        return (lax.rem(row + step, n_row), column)

    def heads_of(part):
        return pl.ds(part[0], part[1])

    own = pltpu.make_async_copy(pkv_hbm.at[0], own_ref, in_sem.at[0])
    own.start()
    barrier = pltpu.get_barrier_semaphore()
    for stride in STRIDES:
        pl.semaphore_signal(barrier, inc=1, device_id=beside(stride), device_id_type=MESH)
    for step in NEAR:
        pl.semaphore_signal(barrier, inc=1, device_id=above(step), device_id_type=MESH)
    loads = []
    for source, target in (
        (owner_hbm, owner_ref),
        (kv_hbm.at[0, 0], kv_ref),
        (q_hbm.at[0, 0], q_ref),
        (g_hbm.at[0, 0], g_ref),
    ):
        loads.append(pltpu.make_async_copy(source, target, in_sem.at[len(loads) + 1]))
        loads[-1].start()
    own.wait()
    for head in range(KVH):
        chunk, part = next((c, p) for c, p in enumerate(PROMPT_PARTS) if p[0] <= head < p[0] + p[1])
        part = land[chunk].at[REACH, head - part[0]]
        part[:, :HD] = own_ref[:, head * HD : (head + 1) * HD]
        part[:, HD:] = own_ref[:, KVW + head * HD : KVW + (head + 1) * HD]
    pl.semaphore_wait(barrier, len(STRIDES) + len(NEAR))

    def to_reader(chunk, index):
        return pltpu.make_async_remote_copy(
            src_ref=land[chunk].at[REACH],
            dst_ref=land[chunk].at[REACH + STRIDES[index]],
            send_sem=s1.at[chunk, index],
            recv_sem=r1.at[chunk, index],
            device_id=beside(STRIDES[index]),
            device_id_type=MESH,
        )

    for chunk in range(len(PROMPT_PARTS)):
        for index in range(len(STRIDES)):
            to_reader(chunk, index).start()
    for step in NEAR:
        pl.semaphore_signal(near_sem, inc=1, device_id=above(step), device_id_type=MESH)
    for load in loads:
        load.wait()

    blocks = lengths_ref[0, 0]
    key_at = lax.broadcasted_iota(jnp.int32, (BLOCK, HALF), 0)
    lane_at = lax.broadcasted_iota(jnp.int32, (BLOCK, HALF), 1)
    seen = key_at <= lax.rem(lane_at, BLOCK)

    def response(head, carry):
        span = pl.ds(pl.multiple_of(head * HALF, HALF), HALF)
        high = g_ref[pl.ds(BLOCK, BLOCK), span]
        g_ref[pl.ds(BLOCK, BLOCK), span] = jnp.where(blocks > 1, high, jnp.zeros_like(high))
        queries = head_rows(q_ref, head)
        out_grads = head_rows(g_ref, head)
        keys = kv_ref[:, columns_of(head, 0)]
        values = kv_ref[:, columns_of(head, KVW)]
        score0 = dot_t(keys[:BLOCK], queries)
        score1 = dot_t(keys[BLOCK:], queries[HALF:])
        low = jnp.where(seen, score0[:, :HALF], LOWEST)
        high0 = score0[:, HALF:]
        high1 = jnp.where(seen, score1, LOWEST)
        top_low = jnp.max(low, axis=0, keepdims=True) * LOG_SCALE
        top_high = (
            jnp.maximum(jnp.max(high0, axis=0, keepdims=True), jnp.max(high1, axis=0, keepdims=True))
            * LOG_SCALE
        )
        low = jnp.exp2(low * LOG_SCALE - top_low)
        high0 = jnp.exp2(high0 * LOG_SCALE - top_high)
        high1 = jnp.exp2(high1 * LOG_SCALE - top_high)
        mass_low = jnp.sum(low, axis=0, keepdims=True)
        mass_high = jnp.sum(high0, axis=0, keepdims=True) + jnp.sum(high1, axis=0, keepdims=True)
        low = low * (1.0 / mass_low)
        inverse = 1.0 / mass_high
        high0 = high0 * inverse
        high1 = high1 * inverse
        back0 = dot_t(values[:BLOCK], out_grads)
        back1 = dot_t(values[BLOCK:], out_grads[HALF:])
        delta_low = jnp.sum(low * back0[:, :HALF], axis=0, keepdims=True)
        delta_high = jnp.sum(high0 * back0[:, HALF:], axis=0, keepdims=True) + jnp.sum(
            high1 * back1, axis=0, keepdims=True
        )
        prob_resp[head, 0] = low
        prob_resp[head, 1] = high0
        prob_resp[head, 2] = high1
        back_resp[head, 0] = back0[:, :HALF]
        back_resp[head, 1] = back0[:, HALF:]
        back_resp[head, 2] = back1
        stats[head, 0:1] = jnp.concatenate([top_low, top_high], axis=1)
        stats[head, 1:2] = jnp.concatenate([mass_low, mass_high], axis=1)
        stats[head, 2:3] = jnp.concatenate([delta_low, delta_high], axis=1)
        return carry

    lax.fori_loop(0, KVH, response, 0)

    wanted = owner_ref[column]
    offset = jnp.minimum(lax.rem(column - wanted + n_col + REACH, n_col), 2 * REACH)
    mine = pl.ds(pl.multiple_of(row * 16, 16), 16)

    def along(chunk, step):
        block = gath.at[heads_of(PROMPT_PARTS[chunk]), mine]
        return pltpu.make_async_remote_copy(
            src_ref=block,
            dst_ref=block,
            send_sem=s2.at[chunk, step],
            recv_sem=r2.at[chunk, step],
            device_id=above(step),
            device_id_type=MESH,
        )

    pl.semaphore_wait(near_sem, len(NEAR))
    for chunk in range(len(PROMPT_PARTS)):
        for index in range(len(STRIDES)):
            to_reader(chunk, index).wait_recv()
        gath[heads_of(PROMPT_PARTS[chunk]), mine] = land[chunk][offset]
        for step in STEPS:
            along(chunk, step).start()

    def to_row(chunk, step):
        target = lax.rem(row + step, n_row)
        return pltpu.make_async_remote_copy(
            src_ref=grads.at[heads_of(GRAD_PARTS[chunk]), pl.ds(pl.multiple_of(target * 16, 16), 16)],
            dst_ref=sums_in.at[step, heads_of(GRAD_PARTS[chunk])],
            send_sem=s3.at[chunk, step],
            recv_sem=r3.at[chunk, step],
            device_id=above(step),
            device_id_type=MESH,
        )

    def prompt(head, carry):
        queries = head_rows(q_ref, head)
        out_grads = head_rows(g_ref, head)
        keys = gath[head, :, :HD]
        values = gath[head, :, HD:]
        score = dot_t(keys, queries)
        top_resp = stats[head, 0:1]
        top = jnp.maximum(jnp.max(score, axis=0, keepdims=True) * LOG_SCALE, top_resp)
        prob = jnp.exp2(score * LOG_SCALE - top)
        mass_resp = jnp.exp2(top_resp - top) * stats[head, 1:2]
        inverse = 1.0 / (mass_resp + jnp.sum(prob, axis=0, keepdims=True))
        share = mass_resp * inverse
        prob = prob * inverse
        back = dot_t(values, out_grads)
        delta = share * stats[head, 2:3] + jnp.sum(prob * back, axis=0, keepdims=True)
        score_grad = (prob * (back - delta)).astype(BF16)
        grads[head, :, :HD] = (dot_n(score_grad, queries) * SCALE).astype(BF16)
        grads[head, :, HD:] = dot_n(prob.astype(BF16), out_grads).astype(BF16)
        sg_prompt[head] = score_grad
        stats[head, 3:4] = share
        stats[head, 4:5] = delta
        return carry

    for chunk, (first, count) in enumerate(PROMPT_PARTS):
        for step in STEPS:
            along(chunk, step).wait_recv()
        for head in range(first, first + count):
            prompt(head, 0)
            for part, (begin, size) in enumerate(GRAD_PARTS):
                if begin + size == head + 1:
                    for step in STEPS:
                        to_row(part, step).start()

    def finish(head, carry):
        queries = head_rows(q_ref, head)
        out_grads = head_rows(g_ref, head)
        keys = kv_ref[:, columns_of(head, 0)]
        prompt_keys = gath[head, :, :HD]
        share = stats[head, 3:4]
        delta = stats[head, 4:5]
        low = prob_resp[head, 0] * share[:, :HALF]
        high0 = prob_resp[head, 1] * share[:, HALF:]
        high1 = prob_resp[head, 2] * share[:, HALF:]
        sg_low = (low * (back_resp[head, 0] - delta[:, :HALF])).astype(BF16)
        sg_high0 = (high0 * (back_resp[head, 1] - delta[:, HALF:])).astype(BF16)
        sg_high1 = (high1 * (back_resp[head, 2] - delta[:, HALF:])).astype(BF16)
        sg0 = jnp.concatenate([sg_low, sg_high0], axis=1)
        pr0 = jnp.concatenate([low.astype(BF16), high0.astype(BF16)], axis=1)
        key_at = columns_of(head, 0)
        value_at = columns_of(head, KVW)
        rg_ref[pl.ds(0, BLOCK), key_at] = (dot_n(sg0, queries) * SCALE).astype(BF16)
        rg_ref[pl.ds(BLOCK, BLOCK), key_at] = (dot_n(sg_high1, queries[HALF:]) * SCALE).astype(BF16)
        rg_ref[pl.ds(0, BLOCK), value_at] = dot_n(pr0, out_grads).astype(BF16)
        rg_ref[pl.ds(BLOCK, BLOCK), value_at] = dot_n(high1.astype(BF16), out_grads[HALF:]).astype(BF16)
        sgp = sg_prompt[head]
        grad_low = dot_l(
            jnp.concatenate([sgp[:, :HALF], sg_low], axis=0),
            jnp.concatenate([prompt_keys, keys[:BLOCK]], axis=0),
        )
        grad_high = dot_l(
            jnp.concatenate([sgp[:, HALF:], sg_high0, sg_high1], axis=0),
            jnp.concatenate([prompt_keys, keys], axis=0),
        )
        for half, grad in enumerate((grad_low, grad_high)):
            grad = (grad * SCALE).astype(BF16)
            for group in range(GROUPS):
                at = pl.ds(pl.multiple_of(head * HALF, HALF) + group * HD, HD)
                qg_ref[pl.ds(half * BLOCK, BLOCK), at] = grad[group * BLOCK : (group + 1) * BLOCK]
        return carry

    lax.fori_loop(0, KVH, finish, 0)

    def to_owner(chunk, index):
        return pltpu.make_async_remote_copy(
            src_ref=sum_out.at[heads_of(SUM_PARTS[chunk])],
            dst_ref=sum_land.at[index, heads_of(SUM_PARTS[chunk])],
            send_sem=s4.at[chunk, index],
            recv_sem=r4.at[chunk, index],
            device_id=beside(STRIDES[index]),
            device_id_type=MESH,
        )

    totals = []
    for chunk, (first, count) in enumerate(SUM_PARTS):
        heads = pl.ds(first, count)
        for part, (begin, size) in enumerate(GRAD_PARTS):
            if first <= begin < first + count:
                for step in STEPS:
                    to_row(part, step).wait_recv()
        total = grads[heads, mine].astype(F32)
        for step in STEPS:
            total = total + sums_in[step, heads].astype(F32)
        sum_out[heads] = total.astype(BF16)
        for index in range(len(STRIDES)):
            to_owner(chunk, index).start()
        totals.append(jnp.where(wanted == column, total, 0.0))
    for chunk in range(len(PROMPT_PARTS)):
        for index in range(len(STRIDES)):
            to_reader(chunk, index).wait_send()
        for step in STEPS:
            along(chunk, step).wait_send()
    for part in range(len(GRAD_PARTS)):
        for step in STEPS:
            to_row(part, step).wait_send()
    for chunk, (first, count) in enumerate(SUM_PARTS):
        total = totals[chunk]
        for index in range(len(STRIDES)):
            to_owner(chunk, index).wait()
        for index, stride in enumerate(STRIDES):
            reads = owner_ref[lax.rem(column - stride + n_col, n_col)] == column
            total = total + jnp.where(reads, sum_land[index, pl.ds(first, count)].astype(F32), 0.0)
        for at in range(count):
            head = first + at
            pg_ref[:, head * HD : (head + 1) * HD] = total[at, :, :HD]
            pg_ref[:, KVW + head * HD : KVW + (head + 1) * HD] = total[at, :, HD:]


def store_kernel(qg_ref, rg_ref, pg_ref, qg_hbm, rg_hbm, pg_hbm, sem):
    stores = [
        pltpu.make_async_copy(qg_ref, qg_hbm.at[0, 0], sem.at[0]),
        pltpu.make_async_copy(rg_ref, rg_hbm.at[0, 0], sem.at[1]),
        pltpu.make_async_copy(pg_ref, pg_hbm.at[0], sem.at[2]),
    ]
    for store in stores:
        store.start()
    for store in stores:
        store.wait()


def shards(queries, resp_kv, out_grad, prompt_kv, prompt_of, lengths):
    in_hbm = pl.BlockSpec(memory_space=pltpu.HBM)
    in_vmem = pl.BlockSpec(memory_space=pltpu.VMEM)
    operands = (lengths, prompt_of, queries, resp_kv, out_grad, prompt_kv)
    operands = (pltpu.with_memory_space_constraint(lengths, pltpu.SMEM),) + tuple(pltpu.with_memory_space_constraint(operand, pltpu.HBM) for operand in operands[1:])
    results = pl.pallas_call(
        kernel,
        out_shape=(
            pltpu.VMEM((RLEN, QW), BF16),
            pltpu.VMEM((RLEN, 2 * KVW), BF16),
            pltpu.VMEM((16, 2 * KVW), F32),
        ),
        in_specs=[pl.BlockSpec(memory_space=pltpu.SMEM)] + [in_hbm] * 5,
        out_specs=(in_vmem,) * 3,
        scratch_shapes=[
            pltpu.SMEM((64,), jnp.int32),
            pltpu.VMEM((RLEN, QW), BF16),
            pltpu.VMEM((RLEN, 2 * KVW), BF16),
            pltpu.VMEM((RLEN, QW), BF16),
            pltpu.VMEM((16, 2 * KVW), BF16),
            [pltpu.VMEM((2 * REACH + 1, part[1], 16, 2 * HD), BF16) for part in PROMPT_PARTS],
            pltpu.VMEM((KVH, PLEN, 2 * HD), BF16),
            pltpu.VMEM((KVH, 3, BLOCK, HALF), F32),
            pltpu.VMEM((KVH, 3, BLOCK, HALF), F32),
            pltpu.VMEM((KVH, 8, LANES), F32),
            pltpu.VMEM((KVH, PLEN, LANES), BF16),
            pltpu.VMEM((KVH, PLEN, 2 * HD), BF16),
            pltpu.VMEM((8, KVH, 16, 2 * HD), BF16),
            pltpu.VMEM((KVH, 16, 2 * HD), BF16),
            pltpu.VMEM((2 * REACH, KVH, 16, 2 * HD), BF16),
            pltpu.SemaphoreType.DMA((6,)),
            pltpu.SemaphoreType.REGULAR,
            pltpu.SemaphoreType.DMA((len(PROMPT_PARTS), 6)),
            pltpu.SemaphoreType.DMA((len(PROMPT_PARTS), 6)),
            pltpu.SemaphoreType.DMA((len(PROMPT_PARTS), 8)),
            pltpu.SemaphoreType.DMA((len(PROMPT_PARTS), 8)),
            pltpu.SemaphoreType.DMA((len(GRAD_PARTS), 8)),
            pltpu.SemaphoreType.DMA((len(GRAD_PARTS), 8)),
            pltpu.SemaphoreType.DMA((len(SUM_PARTS), 6)),
            pltpu.SemaphoreType.DMA((len(SUM_PARTS), 6)),
        ],
        compiler_params=pltpu.CompilerParams(
            collective_id=0, has_side_effects=True, vmem_limit_bytes=40 << 20
        ),
        name="slot_grads",
    )(*operands)
    results = [pltpu.with_memory_space_constraint(result, pltpu.VMEM) for result in results]
    return pl.pallas_call(
        store_kernel,
        out_shape=(
            jax.ShapeDtypeStruct(queries.shape, BF16),
            jax.ShapeDtypeStruct(resp_kv.shape, BF16),
            jax.ShapeDtypeStruct(prompt_kv.shape, F32),
        ),
        in_specs=[in_vmem] * 3,
        out_specs=(in_hbm,) * 3,
        scratch_shapes=[pltpu.SemaphoreType.DMA((3,))],
        name="store",
    )(*results)


def solution(mesh):
    return jax.shard_map(
        shards,
        mesh=mesh,
        in_specs=(
            P("prompt", "resp", None, None),
            P("prompt", "resp", None, None),
            P("prompt", "resp", None, None),
            P("resp", "prompt", None),
            P(),
            P("prompt", "resp"),
        ),
        out_specs=(
            P("prompt", "resp", None, None),
            P("prompt", "resp", None, None),
            P("resp", "prompt", None),
        ),
        check_vma=False,
    )
```

```python
import functools
import math

import jax
import jax.numpy as jnp
from jax import lax
from jax.experimental import pallas as pl
from jax.experimental.pallas import tpu as pltpu
from jax.sharding import PartitionSpec as P

QH = 16
KVH = 4
GROUPS = QH // KVH
HD = 128
BLOCK = 128
REACH = 3
RLEN = 256
PLEN = 128
KVW = KVH * HD
QW = QH * HD
HALF = GROUPS * BLOCK
LANES = 2 * HALF
SCALE = HD**-0.5
LOG_SCALE = SCALE * math.log2(math.e)
CHUNKS = 2
PER = KVH // CHUNKS
STRIDES = (-3, 3, -2, 2, -1, 1)
STEPS = (4, 3, 5, 2, 6, 1, 7)
NEAR = (1, 7, 2, 6)
MESH = pl.DeviceIdType.MESH
F32 = jnp.float32
BF16 = jnp.bfloat16
LOWEST = -3.0e38


def dot_t(a, b):
    return lax.dot_general(a, b, (((1,), (1,)), ((), ())), preferred_element_type=F32)


def dot_n(a, b):
    return lax.dot_general(a, b, (((1,), (0,)), ((), ())), preferred_element_type=F32)


def dot_l(a, b):
    return lax.dot_general(a, b, (((0,), (0,)), ((), ())), preferred_element_type=F32)


def head_rows(ref, head):
    parts = []
    for half in range(2):
        for group in range(GROUPS):
            first = head * HALF if isinstance(head, int) else pl.multiple_of(head * HALF, HALF)
            columns = pl.ds(first + group * HD, HD)
            parts.append(ref[pl.ds(half * BLOCK, BLOCK), columns])
    return jnp.concatenate(parts, axis=0)


def columns_of(head, first):
    return pl.ds(head * HD + first, HD) if isinstance(head, int) else pl.ds(pl.multiple_of(head * HD, HD) + first, HD)


def kernel(
    lengths_ref,
    owner_hbm,
    q_hbm,
    kv_hbm,
    g_hbm,
    pkv_hbm,
    qg_ref,
    rg_ref,
    pg_ref,
    owner_ref,
    q_ref,
    kv_ref,
    g_ref,
    own_ref,
    land0,
    land1,
    gath,
    prob_resp,
    back_resp,
    stats,
    sg_prompt,
    grads,
    sums_in,
    sum_out,
    sum_land,
    in_sem,
    near_sem,
    s1,
    r1,
    s2,
    r2,
    s3,
    r3,
    s4,
    r4,
):
    land = (land0, land1)
    row = lax.axis_index("prompt")
    column = lax.axis_index("resp")
    n_row = lax.axis_size("prompt")
    n_col = lax.axis_size("resp")

    def beside(stride):
        return (row, lax.rem(column + stride + n_col, n_col))

    def above(step):
        return (lax.rem(row + step, n_row), column)

    def heads_of(chunk):
        return pl.ds(chunk * PER, PER)

    own = pltpu.make_async_copy(pkv_hbm.at[0], own_ref, in_sem.at[0])
    own.start()
    barrier = pltpu.get_barrier_semaphore()
    for stride in STRIDES:
        pl.semaphore_signal(barrier, inc=1, device_id=beside(stride), device_id_type=MESH)
    for step in NEAR:
        pl.semaphore_signal(barrier, inc=1, device_id=above(step), device_id_type=MESH)
    loads = []
    for source, target in (
        (owner_hbm, owner_ref),
        (kv_hbm.at[0, 0], kv_ref),
        (q_hbm.at[0, 0], q_ref),
        (g_hbm.at[0, 0], g_ref),
    ):
        loads.append(pltpu.make_async_copy(source, target, in_sem.at[len(loads) + 1]))
        loads[-1].start()
    own.wait()
    for head in range(KVH):
        part = land[head // PER].at[REACH, head % PER]
        part[:, :HD] = own_ref[:, head * HD : (head + 1) * HD]
        part[:, HD:] = own_ref[:, KVW + head * HD : KVW + (head + 1) * HD]
    pl.semaphore_wait(barrier, len(STRIDES) + len(NEAR))

    def to_reader(chunk, index):
        return pltpu.make_async_remote_copy(
            src_ref=land[chunk].at[REACH],
            dst_ref=land[chunk].at[REACH + STRIDES[index]],
            send_sem=s1.at[chunk, index],
            recv_sem=r1.at[chunk, index],
            device_id=beside(STRIDES[index]),
            device_id_type=MESH,
        )

    for chunk in range(CHUNKS):
        for index in range(len(STRIDES)):
            to_reader(chunk, index).start()
    for step in NEAR:
        pl.semaphore_signal(near_sem, inc=1, device_id=above(step), device_id_type=MESH)
    for load in loads:
        load.wait()

    blocks = lengths_ref[0, 0]
    key_at = lax.broadcasted_iota(jnp.int32, (BLOCK, HALF), 0)
    lane_at = lax.broadcasted_iota(jnp.int32, (BLOCK, HALF), 1)
    seen = key_at <= lax.rem(lane_at, BLOCK)

    def response(head, carry):
        span = pl.ds(pl.multiple_of(head * HALF, HALF), HALF)
        high = g_ref[pl.ds(BLOCK, BLOCK), span]
        g_ref[pl.ds(BLOCK, BLOCK), span] = jnp.where(blocks > 1, high, jnp.zeros_like(high))
        queries = head_rows(q_ref, head)
        out_grads = head_rows(g_ref, head)
        keys = kv_ref[:, columns_of(head, 0)]
        values = kv_ref[:, columns_of(head, KVW)]
        score0 = dot_t(keys[:BLOCK], queries)
        score1 = dot_t(keys[BLOCK:], queries[HALF:])
        low = jnp.where(seen, score0[:, :HALF], LOWEST)
        high0 = score0[:, HALF:]
        high1 = jnp.where(seen, score1, LOWEST)
        top_low = jnp.max(low, axis=0, keepdims=True) * LOG_SCALE
        top_high = (
            jnp.maximum(jnp.max(high0, axis=0, keepdims=True), jnp.max(high1, axis=0, keepdims=True))
            * LOG_SCALE
        )
        low = jnp.exp2(low * LOG_SCALE - top_low)
        high0 = jnp.exp2(high0 * LOG_SCALE - top_high)
        high1 = jnp.exp2(high1 * LOG_SCALE - top_high)
        mass_low = jnp.sum(low, axis=0, keepdims=True)
        mass_high = jnp.sum(high0, axis=0, keepdims=True) + jnp.sum(high1, axis=0, keepdims=True)
        low = low * (1.0 / mass_low)
        inverse = 1.0 / mass_high
        high0 = high0 * inverse
        high1 = high1 * inverse
        back0 = dot_t(values[:BLOCK], out_grads)
        back1 = dot_t(values[BLOCK:], out_grads[HALF:])
        delta_low = jnp.sum(low * back0[:, :HALF], axis=0, keepdims=True)
        delta_high = jnp.sum(high0 * back0[:, HALF:], axis=0, keepdims=True) + jnp.sum(
            high1 * back1, axis=0, keepdims=True
        )
        prob_resp[head, 0] = low
        prob_resp[head, 1] = high0
        prob_resp[head, 2] = high1
        back_resp[head, 0] = back0[:, :HALF]
        back_resp[head, 1] = back0[:, HALF:]
        back_resp[head, 2] = back1
        stats[head, 0:1] = jnp.concatenate([top_low, top_high], axis=1)
        stats[head, 1:2] = jnp.concatenate([mass_low, mass_high], axis=1)
        stats[head, 2:3] = jnp.concatenate([delta_low, delta_high], axis=1)
        return carry

    lax.fori_loop(0, KVH, response, 0)

    wanted = owner_ref[column]
    offset = jnp.minimum(lax.rem(column - wanted + n_col + REACH, n_col), 2 * REACH)
    mine = pl.ds(pl.multiple_of(row * 16, 16), 16)

    def along(chunk, step):
        block = gath.at[heads_of(chunk), mine]
        return pltpu.make_async_remote_copy(
            src_ref=block,
            dst_ref=block,
            send_sem=s2.at[chunk, step],
            recv_sem=r2.at[chunk, step],
            device_id=above(step),
            device_id_type=MESH,
        )

    pl.semaphore_wait(near_sem, len(NEAR))
    for chunk in range(CHUNKS):
        for index in range(len(STRIDES)):
            to_reader(chunk, index).wait_recv()
        gath[heads_of(chunk), mine] = land[chunk][offset]
        for step in STEPS:
            along(chunk, step).start()

    def to_row(chunk, step):
        target = lax.rem(row + step, n_row)
        return pltpu.make_async_remote_copy(
            src_ref=grads.at[heads_of(chunk), pl.ds(pl.multiple_of(target * 16, 16), 16)],
            dst_ref=sums_in.at[step, heads_of(chunk)],
            send_sem=s3.at[chunk, step],
            recv_sem=r3.at[chunk, step],
            device_id=above(step),
            device_id_type=MESH,
        )

    def prompt(head, carry):
        queries = head_rows(q_ref, head)
        out_grads = head_rows(g_ref, head)
        keys = gath[head, :, :HD]
        values = gath[head, :, HD:]
        score = dot_t(keys, queries)
        top_resp = stats[head, 0:1]
        top = jnp.maximum(jnp.max(score, axis=0, keepdims=True) * LOG_SCALE, top_resp)
        prob = jnp.exp2(score * LOG_SCALE - top)
        mass_resp = jnp.exp2(top_resp - top) * stats[head, 1:2]
        inverse = 1.0 / (mass_resp + jnp.sum(prob, axis=0, keepdims=True))
        share = mass_resp * inverse
        prob = prob * inverse
        back = dot_t(values, out_grads)
        delta = share * stats[head, 2:3] + jnp.sum(prob * back, axis=0, keepdims=True)
        score_grad = (prob * (back - delta)).astype(BF16)
        grads[head, :, :HD] = (dot_n(score_grad, queries) * SCALE).astype(BF16)
        grads[head, :, HD:] = dot_n(prob.astype(BF16), out_grads).astype(BF16)
        sg_prompt[head] = score_grad
        stats[head, 3:4] = share
        stats[head, 4:5] = delta
        return carry

    for chunk in range(CHUNKS):
        for step in STEPS:
            along(chunk, step).wait_recv()
        for head in range(chunk * PER, (chunk + 1) * PER):
            prompt(head, 0)
        for step in STEPS:
            to_row(chunk, step).start()

    def finish(head, carry):
        queries = head_rows(q_ref, head)
        out_grads = head_rows(g_ref, head)
        keys = kv_ref[:, columns_of(head, 0)]
        prompt_keys = gath[head, :, :HD]
        share = stats[head, 3:4]
        delta = stats[head, 4:5]
        low = prob_resp[head, 0] * share[:, :HALF]
        high0 = prob_resp[head, 1] * share[:, HALF:]
        high1 = prob_resp[head, 2] * share[:, HALF:]
        sg_low = (low * (back_resp[head, 0] - delta[:, :HALF])).astype(BF16)
        sg_high0 = (high0 * (back_resp[head, 1] - delta[:, HALF:])).astype(BF16)
        sg_high1 = (high1 * (back_resp[head, 2] - delta[:, HALF:])).astype(BF16)
        sg0 = jnp.concatenate([sg_low, sg_high0], axis=1)
        pr0 = jnp.concatenate([low.astype(BF16), high0.astype(BF16)], axis=1)
        key_at = columns_of(head, 0)
        value_at = columns_of(head, KVW)
        rg_ref[pl.ds(0, BLOCK), key_at] = (dot_n(sg0, queries) * SCALE).astype(BF16)
        rg_ref[pl.ds(BLOCK, BLOCK), key_at] = (dot_n(sg_high1, queries[HALF:]) * SCALE).astype(BF16)
        rg_ref[pl.ds(0, BLOCK), value_at] = dot_n(pr0, out_grads).astype(BF16)
        rg_ref[pl.ds(BLOCK, BLOCK), value_at] = dot_n(high1.astype(BF16), out_grads[HALF:]).astype(BF16)
        sgp = sg_prompt[head]
        grad_low = dot_l(
            jnp.concatenate([sgp[:, :HALF], sg_low], axis=0),
            jnp.concatenate([prompt_keys, keys[:BLOCK]], axis=0),
        )
        grad_high = dot_l(
            jnp.concatenate([sgp[:, HALF:], sg_high0, sg_high1], axis=0),
            jnp.concatenate([prompt_keys, keys], axis=0),
        )
        for half, grad in enumerate((grad_low, grad_high)):
            grad = (grad * SCALE).astype(BF16)
            for group in range(GROUPS):
                at = pl.ds(pl.multiple_of(head * HALF, HALF) + group * HD, HD)
                qg_ref[pl.ds(half * BLOCK, BLOCK), at] = grad[group * BLOCK : (group + 1) * BLOCK]
        return carry

    lax.fori_loop(0, KVH, finish, 0)

    def to_owner(chunk, index):
        return pltpu.make_async_remote_copy(
            src_ref=sum_out.at[heads_of(chunk)],
            dst_ref=sum_land.at[index, heads_of(chunk)],
            send_sem=s4.at[chunk, index],
            recv_sem=r4.at[chunk, index],
            device_id=beside(STRIDES[index]),
            device_id_type=MESH,
        )

    totals = []
    for chunk in range(CHUNKS):
        total = grads[heads_of(chunk), mine].astype(F32)
        for step in STEPS:
            to_row(chunk, step).wait_recv()
        for step in STEPS:
            total = total + sums_in[step, heads_of(chunk)].astype(F32)
        sum_out[heads_of(chunk)] = total.astype(BF16)
        for index in range(len(STRIDES)):
            to_owner(chunk, index).start()
        totals.append(jnp.where(wanted == column, total, 0.0))
    for chunk in range(CHUNKS):
        for index in range(len(STRIDES)):
            to_reader(chunk, index).wait_send()
        for step in STEPS:
            along(chunk, step).wait_send()
            to_row(chunk, step).wait_send()
    for chunk in range(CHUNKS):
        total = totals[chunk]
        for index in range(len(STRIDES)):
            to_owner(chunk, index).wait()
        for index, stride in enumerate(STRIDES):
            reads = owner_ref[lax.rem(column - stride + n_col, n_col)] == column
            total = total + jnp.where(reads, sum_land[index, heads_of(chunk)].astype(F32), 0.0)
        for at in range(PER):
            head = chunk * PER + at
            pg_ref[:, head * HD : (head + 1) * HD] = total[at, :, :HD]
            pg_ref[:, KVW + head * HD : KVW + (head + 1) * HD] = total[at, :, HD:]


def store_kernel(qg_ref, rg_ref, pg_ref, qg_hbm, rg_hbm, pg_hbm, sem):
    stores = [
        pltpu.make_async_copy(qg_ref, qg_hbm.at[0, 0], sem.at[0]),
        pltpu.make_async_copy(rg_ref, rg_hbm.at[0, 0], sem.at[1]),
        pltpu.make_async_copy(pg_ref, pg_hbm.at[0], sem.at[2]),
    ]
    for store in stores:
        store.start()
    for store in stores:
        store.wait()


def shards(queries, resp_kv, out_grad, prompt_kv, prompt_of, lengths):
    in_hbm = pl.BlockSpec(memory_space=pltpu.HBM)
    in_vmem = pl.BlockSpec(memory_space=pltpu.VMEM)
    operands = (lengths, prompt_of, queries, resp_kv, out_grad, prompt_kv)
    operands = (pltpu.with_memory_space_constraint(lengths, pltpu.SMEM),) + tuple(pltpu.with_memory_space_constraint(operand, pltpu.HBM) for operand in operands[1:])
    results = pl.pallas_call(
        kernel,
        out_shape=(
            pltpu.VMEM((RLEN, QW), BF16),
            pltpu.VMEM((RLEN, 2 * KVW), BF16),
            pltpu.VMEM((16, 2 * KVW), F32),
        ),
        in_specs=[pl.BlockSpec(memory_space=pltpu.SMEM)] + [in_hbm] * 5,
        out_specs=(in_vmem,) * 3,
        scratch_shapes=[
            pltpu.SMEM((64,), jnp.int32),
            pltpu.VMEM((RLEN, QW), BF16),
            pltpu.VMEM((RLEN, 2 * KVW), BF16),
            pltpu.VMEM((RLEN, QW), BF16),
            pltpu.VMEM((16, 2 * KVW), BF16),
            pltpu.VMEM((2 * REACH + 1, PER, 16, 2 * HD), BF16),
            pltpu.VMEM((2 * REACH + 1, PER, 16, 2 * HD), BF16),
            pltpu.VMEM((KVH, PLEN, 2 * HD), BF16),
            pltpu.VMEM((KVH, 3, BLOCK, HALF), F32),
            pltpu.VMEM((KVH, 3, BLOCK, HALF), F32),
            pltpu.VMEM((KVH, 8, LANES), F32),
            pltpu.VMEM((KVH, PLEN, LANES), BF16),
            pltpu.VMEM((KVH, PLEN, 2 * HD), BF16),
            pltpu.VMEM((8, KVH, 16, 2 * HD), BF16),
            pltpu.VMEM((KVH, 16, 2 * HD), BF16),
            pltpu.VMEM((2 * REACH, KVH, 16, 2 * HD), BF16),
            pltpu.SemaphoreType.DMA((6,)),
            pltpu.SemaphoreType.REGULAR,
            pltpu.SemaphoreType.DMA((CHUNKS, 6)),
            pltpu.SemaphoreType.DMA((CHUNKS, 6)),
            pltpu.SemaphoreType.DMA((CHUNKS, 8)),
            pltpu.SemaphoreType.DMA((CHUNKS, 8)),
            pltpu.SemaphoreType.DMA((CHUNKS, 8)),
            pltpu.SemaphoreType.DMA((CHUNKS, 8)),
            pltpu.SemaphoreType.DMA((CHUNKS, 6)),
            pltpu.SemaphoreType.DMA((CHUNKS, 6)),
        ],
        compiler_params=pltpu.CompilerParams(
            collective_id=0, has_side_effects=True, vmem_limit_bytes=40 << 20
        ),
        name="slot_grads",
    )(*operands)
    results = [pltpu.with_memory_space_constraint(result, pltpu.VMEM) for result in results]
    return pl.pallas_call(
        store_kernel,
        out_shape=(
            jax.ShapeDtypeStruct(queries.shape, BF16),
            jax.ShapeDtypeStruct(resp_kv.shape, BF16),
            jax.ShapeDtypeStruct(prompt_kv.shape, F32),
        ),
        in_specs=[in_vmem] * 3,
        out_specs=(in_hbm,) * 3,
        scratch_shapes=[pltpu.SemaphoreType.DMA((3,))],
        name="store",
    )(*results)


def solution(mesh):
    return jax.shard_map(
        shards,
        mesh=mesh,
        in_specs=(
            P("prompt", "resp", None, None),
            P("prompt", "resp", None, None),
            P("prompt", "resp", None, None),
            P("resp", "prompt", None),
            P(),
            P("prompt", "resp"),
        ),
        out_specs=(
            P("prompt", "resp", None, None),
            P("prompt", "resp", None, None),
            P("resp", "prompt", None),
        ),
        check_vma=False,
    )
```
